32 devices in a mesh: grp: 4 (over y, core), dev: 8 (over z, x).
Axes of the slice: x: 2, y: 2, z: 4, core: 2. Of those that a mesh axis runs over, the one named last changes fastest.
Arguments:
- a_blocks: bfloat16 [1024, 7, 128, 128], P(('grp', 'dev')), may hold values from -0.5 to 0.5
- p_blocks: bfloat16 [1024, 128, 128], P(('grp', 'dev')), may hold values from -0.5 to 0.5
- neighbours: int32 [1024, 6], P(('grp', 'dev')), may hold values from 0 to 31
- coarse_slot: int32 [1024, 7], P(('grp', 'dev')), may hold values from 0 to 6
- owner: int32 [1024, 1], P(('grp', 'dev')), may hold values from 0 to 7; in each aligned block of 32 rows (0 to 31, 32 to 63, ...) at most 8 rows name the same one
- agg_local: int32 [1024], P(('grp', 'dev')), may hold values from 0 to 7
Outputs:
- coarse: bfloat16 [256, 7, 128, 128], P(('grp', 'dev'))
The draws below stay inside these ranges and needn't reach their ends.
Inputs may be any that keep to these rules, and one draw needn't show every extreme that they name: Among the elements of one device at most 8 have the same owner, and in every draw some device has exactly 8 elements with one owner.
All inputs are finite; a program needn't handle non-finite values.
Results may differ from the reference program's by a relative error of at most 0.008.
Values may be sent and summed in bfloat16 or wider, within the bound.
No kernel may reach another device: no remote copies, remote signals or barrier semaphores. Data moves between devices by JAX's collectives and lax.ppermute only.
A program may use at most 128 MiB of HBM per device.

```python
import math
import jax
import jax.numpy as jnp
import numpy as np
from jax import lax

BLK = 128
KC = 7
E_DEV = 32
AGG_DEV = 8
CAP = 8
OWNERS = 8
ELEMENTS = 1024
AGGS = 256
N_GRP = 4
N_DEV = 8


def touch_ends(result, rng, least, high):
    extent = result.shape
    spot = [jax.random.randint(jax.random.fold_in(rng, axis), (), 0, extent[axis]) for axis in range(len(extent))]
    result = result.at[tuple(spot)].set(least)
    longest = extent.index(max(extent))
    spot[longest] = (spot[longest] + 1) % extent[longest]
    return result.at[tuple(spot)].set(high)


def levels(key, dims, split, smallest, high):
    gain = 1.0
    for axis_at, blocks in split:
        heights = jax.random.uniform(jax.random.fold_in(jax.random.fold_in(key, 6), axis_at), (blocks,), jnp.float32, smallest / len(split), high / len(split))
        gain = gain * jnp.repeat(jnp.exp(heights), dims[axis_at] // blocks).reshape((-1,) + (1,) * (len(dims) - 1 - axis_at))
    return gain


def assign_block(stream_key, own, number, rows, number_of, top, reach, slope):
    ranking = jax.random.permutation(stream_key, number_of)
    packed, usual = portions_of(number_of, rows * top, reach, slope, True), portions_of(number_of, rows * top, reach, slope, False)
    places = jnp.arange(number_of)

    def named(tallies, offset_by):
        used = int((tallies > 0).sum())
        fixed = max(1, used // 4)
        passed = fixed + (places - fixed + offset_by * (used - fixed)) % max(1, number_of - fixed)
        return jnp.zeros((number_of,), jnp.int32).at[ranking[jnp.where(places < fixed, places, passed)]].set(jnp.asarray(tallies, jnp.int32))

    tallies = jnp.where(number % 4 == 0, named(packed, number // 4), named(usual, number - number // 4 - 1))
    mixed = jax.random.permutation(jax.random.fold_in(own, 3), number_of)
    source_of, sink = mixed[0:number_of // 2 * 2:2], mixed[1:number_of // 2 * 2:2]
    room = jnp.minimum(tallies[source_of] - 1, reach - tallies[sink]) // 2
    room = jnp.where((source_of == ranking[0]) | (sink == ranking[0]) | (tallies[sink] == 0), 0, jnp.maximum(room, 0))
    passed = jax.random.randint(jax.random.fold_in(own, 4), (number_of // 2,), 0, 1 << 20) % (room + 1)
    tallies = tallies.at[source_of].add(-passed).at[sink].add(passed)
    items = jnp.searchsorted(jnp.cumsum(tallies), jnp.arange(rows * top), side="right").astype(jnp.int32)
    table = items.reshape(top, rows).T
    table = table[jax.random.permutation(jax.random.fold_in(own, 1), rows)]
    offset_by = jax.random.randint(jax.random.fold_in(own, 2), (rows, 1), 0, top)
    return jnp.take_along_axis(table, (jnp.arange(top)[None, :] + offset_by) % top, axis=1)


def portions_of(count, total, reach, skew, full):
    portions = [(1 << 20) // math.isqrt(rank ** skew) + 1 for rank in range(1, count + 1)]
    largest = reach if full else min(reach, max(-(-total // count), total * portions[0] // sum(portions)))
    least = 1 if total - largest >= count - 1 else 0
    given, surplus = [largest] + [least] * (count - 1), total - largest - least * (count - 1)
    while surplus > 0:
        movable = [i for i in range(1, count) if given[i] < largest] or [i for i in range(1, count) if given[i] < reach]
        whole, remaining = sum([portions[i] for i in movable]), surplus
        for i in movable:
            extra = min(reach - given[i], max(1, remaining * portions[i] // whole), surplus)
            given[i] = given[i] + extra
            surplus = surplus - extra
    return np.array(given)


def normal_values(own_key, shape, width, most, shards=(), kind=jnp.bfloat16):
    result = jax.random.normal(own_key, shape, jnp.float32) * width
    if len(shards) > 0:
        result = levels(own_key, shape, shards, -0.22, 0.18) * result
    return jnp.clip(result, min=-most, max=most).astype(kind)


def setup_inputs(seed: int = 0) -> dict:
    key_list = jax.random.split(jax.random.key(seed), 7)
    a_blocks = normal_values(key_list[0], (ELEMENTS, 7, BLK, BLK), BLK ** -0.5, 0.5, ((0, 32),))
    p_blocks = normal_values(key_list[1], (ELEMENTS, BLK, BLK), BLK ** -0.5, 0.5, ((0, 32),))
    neighbours = touch_ends(jax.random.randint(key_list[2], (ELEMENTS, 6), 0, E_DEV), jax.random.fold_in(key_list[2], 1), 0, E_DEV - 1).astype(jnp.int32)
    coarse_slot = touch_ends(jax.random.randint(key_list[3], (ELEMENTS, 7), 0, KC), jax.random.fold_in(key_list[3], 1), 0, KC - 1).astype(jnp.int32)
    owner_keys = jax.random.split(jax.random.fold_in(key_list[4], 1), ELEMENTS // E_DEV)
    owner_turns = jax.random.permutation(jax.random.fold_in(key_list[4], 3), ELEMENTS // E_DEV)
    owner = jax.vmap(lambda own, number: assign_block(jax.random.fold_in(key_list[4], 2), own, number, E_DEV, OWNERS, 1, CAP, 2))(owner_keys, owner_turns).reshape((ELEMENTS, 1))
    agg_local = touch_ends(jax.random.randint(key_list[5], (ELEMENTS,), 0, AGG_DEV), jax.random.fold_in(key_list[5], 1), 0, AGG_DEV - 1).astype(jnp.int32)
    return {"a_blocks": a_blocks, "p_blocks": p_blocks, "neighbours": neighbours, "coarse_slot": coarse_slot, "owner": owner, "agg_local": agg_local}


def device_terms(a_dev, p_dev, sources, near_dev, slot_dev):
    faces = [p_dev] + [jnp.take(sources[face], near_dev[:, face], axis=0) for face in range(6)]
    facing = jnp.stack(faces, 1)
    applied = jnp.einsum('efik,efkj->efij', a_dev.astype(jnp.float32), facing.astype(jnp.float32)).astype(jnp.bfloat16)
    weighted = jnp.einsum('eki,efkj->efij', p_dev.astype(jnp.float32), applied.astype(jnp.float32))
    onehot = (slot_dev[:, :, None] == jnp.arange(KC, dtype=jnp.int32)[None, None, :]).astype(jnp.float32)
    return jnp.einsum('efs,efij->esij', onehot, weighted, precision=lax.Precision.HIGHEST)


def reference(a_blocks, p_blocks, neighbours, coarse_slot, owner, agg_local):
    p_all = p_blocks.reshape(N_GRP, N_DEV, E_DEV, BLK, BLK)
    padded = jnp.pad(p_all, ((1, 1), (1, 1), (0, 0), (0, 0), (0, 0)))
    a_all = a_blocks.reshape(N_GRP * N_DEV, E_DEV, 7, BLK, BLK)
    near_all = neighbours.reshape(N_GRP * N_DEV, E_DEV, 6)
    slot_all = coarse_slot.reshape(N_GRP * N_DEV, E_DEV, 7)
    owner_all = owner.reshape(N_GRP * N_DEV, E_DEV)
    local_all = agg_local.reshape(N_GRP * N_DEV, E_DEV)
    order = jnp.arange(E_DEV, dtype=jnp.int32)

    def one_device(total, index):
        grp_i = index // N_DEV
        dev_i = index % N_DEV
        p_dev = padded[grp_i + 1, dev_i + 1]
        sources = (p_dev, p_dev, padded[grp_i + 1, dev_i], padded[grp_i + 1, dev_i + 2],
                   padded[grp_i, dev_i + 1], padded[grp_i + 2, dev_i + 1])
        terms = device_terms(a_all[index], p_dev, sources, near_all[index], slot_all[index])
        targets = ((grp_i * N_DEV + owner_all[index]) * AGG_DEV + local_all[index]).astype(jnp.int32)
        same = targets[:, None] == targets[None, :]
        firstidx = jnp.min(jnp.where(same, order[None, :], E_DEV), 1)
        first = (firstidx == order).astype(jnp.float32)
        summed = jnp.einsum('ab,bsij->asij', same.astype(jnp.float32), terms, precision=lax.Precision.HIGHEST)
        rounded = summed.astype(jnp.bfloat16).astype(jnp.float32) * first[:, None, None, None]
        total = total.at[targets].add(rounded)
        return total, None

    start = jnp.zeros((AGGS, KC, BLK, BLK), jnp.float32)
    total, _ = lax.scan(one_device, start, jnp.arange(N_GRP * N_DEV, dtype=jnp.int32))
    return total.astype(jnp.bfloat16)
```

```python
import functools

import jax
import jax.numpy as jnp
from jax import lax
from jax.experimental import pallas as pl
from jax.experimental.pallas import tpu as pltpu
from jax.sharding import PartitionSpec as P

KC = 7
FACES = 6
VMEM_BYTES = 40 * 1024 * 1024


def ring_order(count):
    nx = 1 << ((count.bit_length() - 1) // 2)
    nz = count // nx
    if nx < 2 or nz < 2 or nz % 2 or nx * nz != count:
        return list(range(count))
    walk = [(z, 0) for z in range(nz)]
    for step, z in enumerate(reversed(range(nz))):
        xs = range(1, nx)
        walk += [(z, x) for x in (xs if step % 2 == 0 else reversed(xs))]
    return [z * nx + x for z, x in walk]


def chunk_kernel(
    distance, rel, agg, near, slot, a_ref, own, below, above, left, right,
    low, high, acc, a_buf, t_buf, picked, sems,
):
    elems = rel.shape[0]
    half = low.shape[0]
    width = own.shape[1]

    def pick(e, count):
        hit = rel[e] == distance

        @pl.when(hit)
        def _():
            picked[count] = e

        return count + hit.astype(jnp.int32)

    count = lax.fori_loop(0, elems, pick, jnp.int32(0))

    def fetch(i, buf):
        return pltpu.make_async_copy(a_ref.at[picked[i]], a_buf.at[buf], sems.at[buf])

    @pl.when(count > 0)
    def _():
        fetch(0, 0).start()

    acc[...] = jnp.zeros_like(acc)
    sources = (own, own, below, above, left, right)

    def element(i, carry):
        buf = lax.rem(i, 2)

        @pl.when(i + 1 < count)
        def _():
            fetch(i + 1, 1 - buf).start()

        e = picked[i]
        fetch(i, buf).wait()
        p_e = own[e]
        for f in range(KC):
            facing = p_e if f == 0 else sources[f - 1][near[e * FACES + f - 1]]
            t_buf[:, f * width : (f + 1) * width] = jnp.dot(
                a_buf[buf, f], facing, preferred_element_type=jnp.float32
            ).astype(jnp.bfloat16)
        weighted = lax.dot_general(
            p_e, t_buf[...], (((0,), (0,)), ((), ())), preferred_element_type=jnp.float32
        )
        a = agg[e]
        for f in range(KC):
            row = a * KC + slot[e * KC + f]
            acc[row] = acc[row] + weighted[:, f * width : (f + 1) * width]
        return carry

    lax.fori_loop(0, count, element, 0)
    for r in range(2 * half):
        out = low if r < half else high
        for s in range(KC):
            out[r % half, s] = acc[r * KC + s].astype(jnp.bfloat16)


def chunk(distance, aggs, tables, a_blocks, blocks):
    elems, _, width, _ = a_blocks.shape
    half = aggs // 2
    out = jax.ShapeDtypeStruct((half, KC, width, width), jnp.bfloat16)
    smem = pl.BlockSpec(memory_space=pltpu.SMEM)
    vmem = pl.BlockSpec(memory_space=pltpu.VMEM)
    return pl.pallas_call(
        functools.partial(chunk_kernel, distance),
        out_shape=(out, out),
        in_specs=[smem] * 4 + [pl.BlockSpec(memory_space=pl.ANY)] + [vmem] * 5,
        out_specs=(vmem, vmem),
        scratch_shapes=[
            pltpu.VMEM((aggs * KC, width, width), jnp.float32),
            pltpu.VMEM((2, KC, width, width), jnp.bfloat16),
            pltpu.VMEM((width, KC * width), jnp.bfloat16),
            pltpu.SMEM((elems,), jnp.int32),
            pltpu.SemaphoreType.DMA((2,)),
        ],
        compiler_params=pltpu.CompilerParams(vmem_limit_bytes=VMEM_BYTES),
        cost_estimate=pl.CostEstimate(
            flops=4 * KC * width**3 * 4, bytes_accessed=12 * 1024 * 1024, transcendentals=0
        ),
    )(*tables, a_blocks, *blocks)


def add(*terms):
    return sum(t.astype(jnp.float32) for t in terms).astype(jnp.bfloat16)


def on_device(a_blocks, p_blocks, neighbours, coarse_slot, owner, agg_local):
    elems = p_blocks.shape[0]
    aggs = elems // 4
    count = lax.axis_size("dev")

    halo = []
    for axis in ("dev", "grp"):
        size = lax.axis_size(axis)
        forward = [(i, i + 1) for i in range(size - 1)]
        backward = [(b, a) for a, b in forward]
        halo += [lax.ppermute(p_blocks, axis, forward), lax.ppermute(p_blocks, axis, backward)]
    blocks = (p_blocks, *halo)

    order = ring_order(count)
    place = [order.index(d) for d in range(count)]
    index = jnp.arange(count, dtype=jnp.int32)
    places = jnp.array(place, jnp.int32)
    mine = jnp.sum(jnp.where(index == lax.axis_index("dev"), places, 0))
    theirs = jnp.sum(jnp.where(owner == index[None, :], places[None, :], 0), 1)
    rel = lax.rem(theirs - mine + count, count)
    tables = (rel, agg_local, neighbours.reshape(-1), coarse_slot.reshape(-1))

    chunks = {}

    def part(distance, side):
        distance %= count
        if distance not in chunks:
            chunks[distance] = chunk(distance, aggs, tables, a_blocks, blocks)
        return chunks[distance][side]

    right = [(order[i], order[(i + 1) % count]) for i in range(count)]
    left = [(b, a) for a, b in right]
    far = count // 2
    got = {}
    for n in range(2 * far - 1):
        distance = far - (n + 1) // 2
        for sign, perm in ((1, right), (-1, left)):
            side = n % 2 if sign > 0 else 1 - n % 2
            terms = [part(sign * distance, side)]
            if n >= 2:
                terms.append(got[sign, n - 2])
            got[sign, n] = lax.ppermute(terms[0] if n < 2 else add(*terms), "dev", perm)
    last = 2 * far - 2
    low = add(part(0, 0), got[1, last], got[-1, last - 1])
    high = add(part(0, 1), got[1, last - 1], got[-1, last])
    return jnp.concatenate([low, high], 0)


def solution(mesh):
    placed = (
        P(("grp", "dev"), None, None, None),
        P(("grp", "dev"), None, None),
        P(("grp", "dev"), None),
        P(("grp", "dev"), None),
        P(("grp", "dev"), None),
        P(("grp", "dev")),
    )
    return jax.shard_map(
        on_device,
        mesh=mesh,
        in_specs=placed,
        out_specs=P(("grp", "dev"), None, None, None),
        check_vma=False,
    )
```

```python
import functools

import jax
import jax.numpy as jnp
from jax import lax
from jax.experimental import pallas as pl
from jax.experimental.pallas import tpu as pltpu
from jax.sharding import PartitionSpec as P

KC = 7
FACES = 6
VMEM_BYTES = 56 * 1024 * 1024


def ring_order(count):
    nx = 1 << ((count.bit_length() - 1) // 2)
    nz = count // nx
    if nx < 2 or nz < 2 or nz % 2 or nx * nz != count:
        return list(range(count))
    walk = [(z, 0) for z in range(nz)]
    for step, z in enumerate(reversed(range(nz))):
        xs = range(1, nx)
        walk += [(z, x) for x in (xs if step % 2 == 0 else reversed(xs))]
    return [z * nx + x for z, x in walk]


def chunk_kernel(
    distance, places, owner, agg, near, slot, a_ref, own, below, above, left, right,
    low, high, acc, a_buf, p_buf, t_buf, picked, sems,
):
    elems, count_dev = owner.shape[0], places.shape[0]
    aggs, _, half, width = low.shape
    depth = a_buf.shape[0]
    sources = (own, own, below, above, left, right)

    target = lax.rem(places[lax.axis_index("dev")] + distance, count_dev)

    def pick(e, count):
        hit = places[owner[e, 0]] == target

        @pl.when(hit)
        def _():
            picked[count] = e

        return count + hit.astype(jnp.int32)

    count = lax.fori_loop(0, elems, pick, jnp.int32(0))

    def fetches(i):
        e, buf = picked[i], lax.rem(i, depth)
        copies = [pltpu.make_async_copy(a_ref.at[e], a_buf.at[buf], sems.at[buf, 0])]
        for f in range(KC):
            source = own.at[e] if f == 0 else sources[f - 1].at[near[e, f - 1]]
            copies.append(pltpu.make_async_copy(source, p_buf.at[buf, f], sems.at[buf, f + 1]))
        return copies

    def start(i):
        @pl.when(i < count)
        def _():
            for copy in fetches(i):
                copy.start()

    for i in range(depth - 1):
        start(i)
    acc[...] = jnp.zeros_like(acc)

    def element(i, carry):
        start(i + depth - 1)
        e, buf = picked[i], lax.rem(i, depth)
        for copy in fetches(i):
            copy.wait()
        for f in range(KC):
            t_buf[:, f * width : (f + 1) * width] = jnp.dot(
                a_buf[buf, f], p_buf[buf, f], preferred_element_type=jnp.float32
            ).astype(jnp.bfloat16)
        weighted = lax.dot_general(
            p_buf[buf, 0], t_buf[...], (((0,), (0,)), ((), ())), preferred_element_type=jnp.float32
        )
        a = agg[e]
        for f in range(KC):
            row = a * KC + slot[e, f]
            acc[row] = acc[row] + weighted[:, f * width : (f + 1) * width]
        return carry

    lax.fori_loop(0, count, element, 0)

    def store(r, carry):
        for s in range(KC):
            block = acc[r * KC + s].astype(jnp.bfloat16)
            low[r, s] = block[:half]
            high[r, s] = block[half:]
        return carry

    lax.fori_loop(0, aggs, store, 0)


def chunk(distance, aggs, tables, a_blocks, blocks):
    elems, _, width, _ = a_blocks.shape
    out = jax.ShapeDtypeStruct((aggs, KC, width // 2, width), jnp.bfloat16)
    smem = pl.BlockSpec(memory_space=pltpu.SMEM)
    vmem = pl.BlockSpec(memory_space=pltpu.VMEM)
    hbm = pl.BlockSpec(memory_space=pl.ANY)
    depth = 4
    return pl.pallas_call(
        functools.partial(chunk_kernel, distance),
        out_shape=(out, out),
        in_specs=[smem] * 5 + [hbm] * 6,
        out_specs=(vmem, vmem),
        scratch_shapes=[
            pltpu.VMEM((aggs * KC, width, width), jnp.float32),
            pltpu.VMEM((depth, KC, width, width), jnp.bfloat16),
            pltpu.VMEM((depth, KC, width, width), jnp.bfloat16),
            pltpu.VMEM((width, KC * width), jnp.bfloat16),
            pltpu.SMEM((elems,), jnp.int32),
            pltpu.SemaphoreType.DMA((depth, KC + 1)),
        ],
        compiler_params=pltpu.CompilerParams(vmem_limit_bytes=VMEM_BYTES),
        cost_estimate=pl.CostEstimate(
            flops=4 * KC * width**3 * 4, bytes_accessed=12 * 1024 * 1024, transcendentals=0
        ),
    )(*tables, a_blocks, *blocks)


def add(*terms):
    return sum(t.astype(jnp.float32) for t in terms).astype(jnp.bfloat16)


def on_device(a_blocks, p_blocks, neighbours, coarse_slot, owner, agg_local):
    elems = p_blocks.shape[0]
    aggs = elems // 4
    count = lax.axis_size("dev")

    order = ring_order(count)
    places = jnp.array([order.index(d) for d in range(count)], jnp.int32)
    tables = (places, owner, agg_local, neighbours, coarse_slot)

    halo = []
    for axis in ("dev", "grp"):
        size = lax.axis_size(axis)
        forward = [(i, i + 1) for i in range(size - 1)]
        backward = [(b, a) for a, b in forward]
        halo += [lax.ppermute(p_blocks, axis, forward), lax.ppermute(p_blocks, axis, backward)]
    blocks = (p_blocks, *halo)
    blocks = lax.optimization_barrier(blocks)

    chunks = {}

    def part(distance, side):
        distance %= count
        if distance not in chunks:
            chunks[distance] = chunk(distance, aggs, tables, a_blocks, blocks)
        return chunks[distance][side]

    right = [(order[i], order[(i + 1) % count]) for i in range(count)]
    left = [(b, a) for a, b in right]
    far = count // 2
    got = {}
    for n in range(2 * far - 1):
        distance = far - (n + 1) // 2
        for sign, perm in ((1, right), (-1, left)):
            side = n % 2 if sign > 0 else 1 - n % 2
            terms = [part(sign * distance, side)]
            if n >= 2:
                terms.append(got[sign, n - 2])
            got[sign, n] = lax.ppermute(terms[0] if n < 2 else add(*terms), "dev", perm)
    last = 2 * far - 2
    low = add(part(0, 0), got[1, last], got[-1, last - 1])
    high = add(part(0, 1), got[1, last - 1], got[-1, last])
    return jnp.concatenate([low, high], 2)


def solution(mesh):
    placed = (
        P(("grp", "dev"), None, None, None),
        P(("grp", "dev"), None, None),
        P(("grp", "dev"), None),
        P(("grp", "dev"), None),
        P(("grp", "dev"), None),
        P(("grp", "dev")),
    )
    return jax.shard_map(
        on_device,
        mesh=mesh,
        in_specs=placed,
        out_specs=P(("grp", "dev"), None, None, None),
        check_vma=False,
    )
```

```python
import functools

import jax
import jax.numpy as jnp
from jax import lax
from jax.experimental import pallas as pl
from jax.experimental.pallas import tpu as pltpu
from jax.sharding import PartitionSpec as P

KC = 7
FACES = 6
VMEM_BYTES = 56 * 1024 * 1024


def columns(count):
    return 1 << ((count.bit_length() - 1) // 2)


def ring_order(count):
    nx = columns(count)
    nz = count // nx
    if nx < 2 or nz < 2 or nz % 2 or nx * nz != count:
        return list(range(count))
    walk = [(z, 0) for z in range(nz)]
    for step, z in enumerate(reversed(range(nz))):
        xs = range(1, nx)
        walk += [(z, x) for x in (xs if step % 2 == 0 else reversed(xs))]
    return [z * nx + x for z, x in walk]


def halo_dev(p_blocks, count):
    if columns(count) != 2:
        forward = [(i, i + 1) for i in range(count - 1)]
        backward = [(b, a) for a, b in forward]
        return (
            (0, p_blocks.shape[0]),
            [lax.ppermute(p_blocks, "dev", backward)],
            [lax.ppermute(p_blocks, "dev", forward)],
        )
    elems = p_blocks.shape[0]
    cuts = (0, 3 * elems // 8, 3 * elems // 4, elems)
    swap = [(i, i ^ 1) for i in range(count)]
    relay = [(i, i + 2) for i in range(0, count - 2, 2)] + [(i, i - 2) for i in range(3, count, 2)]
    straight = [(i, i - 1) for i in range(2, count, 2)] + [(i, i + 1) for i in range(1, count - 1, 2)]
    first, second = [], []
    for low, high in zip(cuts, cuts[1:]):
        piece = p_blocks[low:high]
        if first:
            piece, _ = lax.optimization_barrier((piece, first[-1]))
        first.append(lax.ppermute(piece, "dev", swap))
        if high < elems:
            second.append(lax.ppermute(first[-1], "dev", relay))
        else:
            second.append(lax.ppermute(piece, "dev", straight))
    return cuts, first, second


def chunk_kernel(distance, cuts, places, owner, agg, near, slot, a_ref, own, *refs):
    pieces = len(cuts) - 1
    first, second, (left, right) = refs[:pieces], refs[pieces : 2 * pieces], refs[2 * pieces : 2 * pieces + 2]
    low, high, acc, a_buf, p_buf, t_buf, picked, sems = refs[2 * pieces + 2 :]
    elems, count_dev = owner.shape[0], places.shape[0]
    aggs, _, half, width = low.shape
    depth = a_buf.shape[0]
    me = lax.axis_index("dev")
    odd = lax.rem(me, 2) if pieces > 1 else 0

    target = lax.rem(places[me] + distance, count_dev)

    def pick(e, count):
        hit = places[owner[e, 0]] == target

        @pl.when(hit)
        def _():
            picked[count] = e

        return count + hit.astype(jnp.int32)

    count = lax.fori_loop(0, elems, pick, jnp.int32(0))

    def fetch(source, buf, f):
        return pltpu.make_async_copy(source, p_buf.at[buf, f], sems.at[buf, f])

    def start(i):
        @pl.when(i < count)
        def _():
            e, buf = picked[i], lax.rem(i, depth)
            pltpu.make_async_copy(a_ref.at[e], a_buf.at[buf], sems.at[buf, KC]).start()
            fetch(own.at[e], buf, 0).start()
            for f, source in ((1, own), (2, own), (5, left), (6, right)):
                fetch(source.at[near[e, f - 1]], buf, f).start()
            for f, parts in ((4 - odd, first), (3 + odd, second)):
                n = near[e, f - 1]
                for part, at, end in zip(parts, cuts, cuts[1:]):

                    @pl.when((n >= at) & (n < end))
                    def _():
                        fetch(part.at[n - at], buf, f).start()

    for i in range(depth - 1):
        start(i)
    acc[...] = jnp.zeros_like(acc)

    def element(i, carry):
        start(i + depth - 1)
        e, buf = picked[i], lax.rem(i, depth)
        pltpu.make_async_copy(a_ref.at[e], a_buf.at[buf], sems.at[buf, KC]).wait()
        for f in range(KC):
            fetch(own.at[e], buf, f).wait()
        for f in range(KC):
            t_buf[:, f * width : (f + 1) * width] = jnp.dot(
                a_buf[buf, f], p_buf[buf, f], preferred_element_type=jnp.float32
            ).astype(jnp.bfloat16)
        weighted = lax.dot_general(
            p_buf[buf, 0], t_buf[...], (((0,), (0,)), ((), ())), preferred_element_type=jnp.float32
        )
        a = agg[e]
        for f in range(KC):
            row = a * KC + slot[e, f]
            acc[row] = acc[row] + weighted[:, f * width : (f + 1) * width]
        return carry

    lax.fori_loop(0, count, element, 0)

    def store(r, carry):
        for s in range(KC):
            block = acc[r * KC + s].astype(jnp.bfloat16)
            low[r, s] = block[:half]
            high[r, s] = block[half:]
        return carry

    lax.fori_loop(0, aggs, store, 0)


def chunk(distance, aggs, cuts, tables, a_blocks, blocks):
    elems, _, width, _ = a_blocks.shape
    out = jax.ShapeDtypeStruct((aggs, KC, width // 2, width), jnp.bfloat16)
    smem = pl.BlockSpec(memory_space=pltpu.SMEM)
    vmem = pl.BlockSpec(memory_space=pltpu.VMEM)
    hbm = pl.BlockSpec(memory_space=pl.ANY)
    depth = 4
    return pl.pallas_call(
        functools.partial(chunk_kernel, distance, cuts),
        out_shape=(out, out),
        in_specs=[smem] * 5 + [hbm] * (1 + len(blocks)),
        out_specs=(vmem, vmem),
        scratch_shapes=[
            pltpu.VMEM((aggs * KC, width, width), jnp.float32),
            pltpu.VMEM((depth, KC, width, width), jnp.bfloat16),
            pltpu.VMEM((depth, KC, width, width), jnp.bfloat16),
            pltpu.VMEM((width, KC * width), jnp.bfloat16),
            pltpu.SMEM((elems,), jnp.int32),
            pltpu.SemaphoreType.DMA((depth, KC + 1)),
        ],
        compiler_params=pltpu.CompilerParams(vmem_limit_bytes=VMEM_BYTES),
        cost_estimate=pl.CostEstimate(
            flops=4 * KC * width**3 * 4, bytes_accessed=12 * 1024 * 1024, transcendentals=0
        ),
    )(*tables, a_blocks, *blocks)


def add(*terms):
    return sum(t.astype(jnp.float32) for t in terms).astype(jnp.bfloat16)


def on_device(a_blocks, p_blocks, neighbours, coarse_slot, owner, agg_local):
    elems = p_blocks.shape[0]
    aggs = elems // 4
    count = lax.axis_size("dev")

    order = ring_order(count)
    places = jnp.array([order.index(d) for d in range(count)], jnp.int32)
    tables = (places, owner, agg_local, neighbours, coarse_slot)

    cuts, first, second = halo_dev(p_blocks, count)
    size = lax.axis_size("grp")
    forward = [(i, i + 1) for i in range(size - 1)]
    backward = [(b, a) for a, b in forward]
    left, right = lax.ppermute(p_blocks, "grp", forward), lax.ppermute(p_blocks, "grp", backward)
    blocks = lax.optimization_barrier((p_blocks, *first, *second, left, right))

    chunks = {}

    def part(distance, side):
        distance %= count
        if distance not in chunks:
            chunks[distance] = chunk(distance, aggs, cuts, tables, a_blocks, blocks)
        return chunks[distance][side]

    right = [(order[i], order[(i + 1) % count]) for i in range(count)]
    left = [(b, a) for a, b in right]
    far = count // 2
    got = {}
    for n in range(2 * far - 1):
        distance = far - (n + 1) // 2
        for sign, perm in ((1, right), (-1, left)):
            side = n % 2 if sign > 0 else 1 - n % 2
            terms = [part(sign * distance, side)]
            if n >= 2:
                terms.append(got[sign, n - 2])
            got[sign, n] = lax.ppermute(terms[0] if n < 2 else add(*terms), "dev", perm)
    last = 2 * far - 2
    low = add(part(0, 0), got[1, last], got[-1, last - 1])
    high = add(part(0, 1), got[1, last - 1], got[-1, last])
    return jnp.concatenate([low, high], 2)


def solution(mesh):
    placed = (
        P(("grp", "dev"), None, None, None),
        P(("grp", "dev"), None, None),
        P(("grp", "dev"), None),
        P(("grp", "dev"), None),
        P(("grp", "dev"), None),
        P(("grp", "dev")),
    )
    return jax.shard_map(
        on_device,
        mesh=mesh,
        in_specs=placed,
        out_specs=P(("grp", "dev"), None, None, None),
        check_vma=False,
    )
```

```python
import functools

import jax
import jax.numpy as jnp
from jax import lax
from jax.experimental import pallas as pl
from jax.experimental.pallas import tpu as pltpu
from jax.sharding import PartitionSpec as P

KC = 7
GROUP = 2
VMEM_BYTES = 56 * 1024 * 1024


def columns(count):
    return 1 << ((count.bit_length() - 1) // 2)


def ring_order(count):
    nx = columns(count)
    nz = count // nx
    if nx < 2 or nz < 2 or nz % 2 or nx * nz != count:
        return list(range(count))
    walk = [(z, 0) for z in range(nz)]
    for step, z in enumerate(reversed(range(nz))):
        xs = range(1, nx)
        walk += [(z, x) for x in (xs if step % 2 == 0 else reversed(xs))]
    return [z * nx + x for z, x in walk]


def halo_dev(p_blocks, count):
    if columns(count) != 2:
        forward = [(i, i + 1) for i in range(count - 1)]
        backward = [(b, a) for a, b in forward]
        return (
            (0, p_blocks.shape[0]),
            [lax.ppermute(p_blocks, "dev", backward)],
            [lax.ppermute(p_blocks, "dev", forward)],
        )
    elems = p_blocks.shape[0]
    cuts = (0, 17 * elems // 32, 25 * elems // 32, elems)
    swap = [(i, i ^ 1) for i in range(count)]
    relay = [(i, i + 2) for i in range(0, count - 2, 2)] + [(i, i - 2) for i in range(3, count, 2)]
    straight = [(i, i - 1) for i in range(2, count, 2)] + [(i, i + 1) for i in range(1, count - 1, 2)]
    first, second = [], []
    for low, high in zip(cuts, cuts[1:]):
        piece = p_blocks[low:high]
        if first:
            piece, _ = lax.optimization_barrier((piece, first[-1]))
        first.append(lax.ppermute(piece, "dev", swap))
        if high < elems:
            second.append(lax.ppermute(first[-1], "dev", relay))
        else:
            second.append(lax.ppermute(piece, "dev", straight))
    return cuts, first, second


def chunk_kernel(distance, cuts, places, owner, agg, near, slot, a_ref, own, *refs):
    pieces = len(cuts) - 1
    first, second, (left, right) = refs[:pieces], refs[pieces : 2 * pieces], refs[2 * pieces : 2 * pieces + 2]
    low, high, acc, a_buf, p_buf, t_buf, halves, picked, sems, out_sems = refs[2 * pieces + 2 :]
    elems, count_dev = owner.shape[1], places.shape[0]
    aggs, _, half, width = low.shape
    depth = a_buf.shape[0]
    me = lax.axis_index("dev")
    odd = lax.rem(me, 2) if pieces > 1 else 0
    target = lax.rem(places[me] + distance, count_dev)

    def pick(e, count):
        picked[count] = e
        return count + (places[owner[0, e]] == target).astype(jnp.int32)

    count = lax.fori_loop(0, elems, pick, jnp.int32(0), unroll=4)

    def fetch(source, buf, f):
        return pltpu.make_async_copy(source, p_buf.at[buf, f], sems.at[buf, f])

    def fetch_a(e, buf):
        return pltpu.make_async_copy(a_ref.at[e], a_buf.at[buf], sems.at[buf, KC])

    def start(i):
        @pl.when(i < count)
        def _():
            e, buf = picked[i], lax.rem(i, depth)
            fetch_a(e, buf).start()
            fetch(own.at[e], buf, 0).start()
            for f, source in ((1, own), (2, own), (5, left), (6, right)):
                fetch(source.at[near[f - 1, e]], buf, f).start()
            for f, parts in ((4 - odd, first), (3 + odd, second)):
                n = near[f - 1, e]
                for part, at, end in zip(parts, cuts, cuts[1:]):

                    @pl.when((n >= at) & (n < end))
                    def _():
                        fetch(part.at[n - at], buf, f).start()

    for i in range(depth - GROUP):
        start(i)
    acc[...] = jnp.zeros_like(acc)

    def group(g, carry):
        for u in range(GROUP):
            start(g * GROUP + u + depth - GROUP)
        for u in range(GROUP):
            buf = lax.rem(g * GROUP + u, depth)

            @pl.when(g * GROUP + u < count)
            def _():
                fetch_a(0, buf).wait()
                for f in range(KC):
                    fetch(own.at[0], buf, f).wait()

        for u in range(GROUP):
            buf = lax.rem(g * GROUP + u, depth)
            for f in range(KC):
                t_buf[u, :, f * width : (f + 1) * width] = jnp.dot(
                    a_buf[buf, f], p_buf[buf, f], preferred_element_type=jnp.float32
                ).astype(jnp.bfloat16)
        weighted = [
            lax.dot_general(
                p_buf[lax.rem(g * GROUP + u, depth), 0], t_buf[u], (((0,), (0,)), ((), ())),
                preferred_element_type=jnp.float32,
            )
            for u in range(GROUP)
        ]
        for u in range(GROUP):
            i = g * GROUP + u

            @pl.when(i < count)
            def _():
                e = picked[i]
                a = agg[e]
                for f in range(KC):
                    row = a * KC + slot[f, e]
                    acc[row] = acc[row] + weighted[u][:, f * width : (f + 1) * width]

        return carry

    lax.fori_loop(0, (count + GROUP - 1) // GROUP, group, 0)

    def moves(r):
        return [
            pltpu.make_async_copy(halves.at[h, r], out.at[r], out_sems.at[h, r])
            for h, out in ((0, low), (1, high))
        ]

    def store(r, carry):
        for s in range(KC):
            block = acc[r * KC + s].astype(jnp.bfloat16)
            halves[0, r, s] = block[:half]
            halves[1, r, s] = block[half:]
        for move in moves(r):
            move.start()
        return carry

    lax.fori_loop(0, aggs, store, 0)

    def finish(r, carry):
        for move in moves(r):
            move.wait()
        return carry

    lax.fori_loop(0, aggs, finish, 0)


def chunk(distance, aggs, cuts, tables, a_blocks, blocks):
    elems, _, width, _ = a_blocks.shape
    out = jax.ShapeDtypeStruct((aggs, KC, width // 2, width), jnp.bfloat16)
    smem = pl.BlockSpec(memory_space=pltpu.SMEM)
    hbm = pl.BlockSpec(memory_space=pl.ANY)
    depth = 3 * GROUP
    return pl.pallas_call(
        functools.partial(chunk_kernel, distance, cuts),
        out_shape=(out, out),
        in_specs=[smem] * len(tables) + [hbm] * (1 + len(blocks)),
        out_specs=(hbm, hbm),
        scratch_shapes=[
            pltpu.VMEM((aggs * KC, width, width), jnp.float32),
            pltpu.VMEM((depth, KC, width, width), jnp.bfloat16),
            pltpu.VMEM((depth, KC, width, width), jnp.bfloat16),
            pltpu.VMEM((GROUP, width, KC * width), jnp.bfloat16),
            pltpu.VMEM((2, aggs, KC, width // 2, width), jnp.bfloat16),
            pltpu.SMEM((elems + 1,), jnp.int32),
            pltpu.SemaphoreType.DMA((depth, KC + 1)),
            pltpu.SemaphoreType.DMA((2, aggs)),
        ],
        compiler_params=pltpu.CompilerParams(vmem_limit_bytes=VMEM_BYTES),
        cost_estimate=pl.CostEstimate(
            flops=4 * KC * width**3 * 4, bytes_accessed=12 * 1024 * 1024, transcendentals=0
        ),
    )(*tables, a_blocks, *blocks)


def add(*terms):
    return sum(t.astype(jnp.float32) for t in terms).astype(jnp.bfloat16)


def on_device(a_blocks, p_blocks, neighbours, coarse_slot, owner, agg_local):
    elems = p_blocks.shape[0]
    aggs = elems // 4
    count = lax.axis_size("dev")

    order = ring_order(count)
    places = jnp.array([order.index(d) for d in range(count)], jnp.int32)
    tables = (places, owner.T, agg_local, neighbours.T, coarse_slot.T)

    cuts, first, second = halo_dev(p_blocks, count)
    size = lax.axis_size("grp")
    forward = [(i, i + 1) for i in range(size - 1)]
    backward = [(b, a) for a, b in forward]
    left, right = lax.ppermute(p_blocks, "grp", forward), lax.ppermute(p_blocks, "grp", backward)
    blocks = lax.optimization_barrier((p_blocks, *first, *second, left, right))

    chunks = {}

    def part(distance, side):
        distance %= count
        if distance not in chunks:
            chunks[distance] = chunk(distance, aggs, cuts, tables, a_blocks, blocks)
        return chunks[distance][side]

    right = [(order[i], order[(i + 1) % count]) for i in range(count)]
    left = [(b, a) for a, b in right]
    far = count // 2
    got = {}
    for n in range(2 * far - 1):
        distance = far - (n + 1) // 2
        for sign, perm in ((1, right), (-1, left)):
            side = n % 2 if sign > 0 else 1 - n % 2
            terms = [part(sign * distance, side)]
            if n >= 2:
                terms.append(got[sign, n - 2])
            got[sign, n] = lax.ppermute(terms[0] if n < 2 else add(*terms), "dev", perm)
    last = 2 * far - 2
    low = add(part(0, 0), got[1, last], got[-1, last - 1])
    high = add(part(0, 1), got[1, last - 1], got[-1, last])
    return jnp.concatenate([low, high], 2)


def solution(mesh):
    placed = (
        P(("grp", "dev"), None, None, None),
        P(("grp", "dev"), None, None),
        P(("grp", "dev"), None),
        P(("grp", "dev"), None),
        P(("grp", "dev"), None),
        P(("grp", "dev")),
    )
    return jax.shard_map(
        on_device,
        mesh=mesh,
        in_specs=placed,
        out_specs=P(("grp", "dev"), None, None, None),
        check_vma=False,
    )
```

```python
import functools

import jax
import jax.numpy as jnp
from jax import lax
from jax.experimental import pallas as pl
from jax.experimental.pallas import tpu as pltpu
from jax.sharding import PartitionSpec as P

KC = 7
GROUP = 2
VMEM_BYTES = 56 * 1024 * 1024


def columns(count):
    return 1 << ((count.bit_length() - 1) // 2)


def ring_order(count):
    nx = columns(count)
    nz = count // nx
    if nx < 2 or nz < 2 or nz % 2 or nx * nz != count:
        return list(range(count))
    walk = [(z, 0) for z in range(nz)]
    for step, z in enumerate(reversed(range(nz))):
        xs = range(1, nx)
        walk += [(z, x) for x in (xs if step % 2 == 0 else reversed(xs))]
    return [z * nx + x for z, x in walk]


def halo_dev(p_blocks, count):
    if columns(count) != 2:
        forward = [(i, i + 1) for i in range(count - 1)]
        backward = [(b, a) for a, b in forward]
        return (
            (0, p_blocks.shape[0]),
            [lax.ppermute(p_blocks, "dev", backward)],
            [lax.ppermute(p_blocks, "dev", forward)],
        )
    elems = p_blocks.shape[0]
    cuts = (0, 16 * elems // 32, 25 * elems // 32, elems)
    swap = [(i, i ^ 1) for i in range(count)]
    relay = [(i, i + 2) for i in range(0, count - 2, 2)] + [(i, i - 2) for i in range(3, count, 2)]
    straight = [(i, i - 1) for i in range(2, count, 2)] + [(i, i + 1) for i in range(1, count - 1, 2)]
    first, second = [], []
    for low, high in zip(cuts, cuts[1:]):
        piece = p_blocks[low:high]
        if first:
            piece, _ = lax.optimization_barrier((piece, first[-1]))
        first.append(lax.ppermute(piece, "dev", swap))
        if high < elems:
            second.append(lax.ppermute(first[-1], "dev", relay))
        else:
            second.append(lax.ppermute(piece, "dev", straight))
    return cuts, first, second


def chunk_kernel(distance, cuts, places, owner, agg, near, slot, a_ref, own, *refs):
    pieces = len(cuts) - 1
    first, second, (left, right) = refs[:pieces], refs[pieces : 2 * pieces], refs[2 * pieces : 2 * pieces + 2]
    low, high, acc, a_buf, p_buf, t_buf, halves, picked, sems, out_sems = refs[2 * pieces + 2 :]
    elems, count_dev = owner.shape[1], places.shape[0]
    aggs, _, half, width = low.shape
    depth = a_buf.shape[0]
    me = lax.axis_index("dev")
    odd = lax.rem(me, 2) if pieces > 1 else 0
    target = lax.rem(places[me] + distance, count_dev)

    def pick(e, count):
        picked[count] = e
        return count + (places[owner[0, e]] == target).astype(jnp.int32)

    count = lax.fori_loop(0, elems, pick, jnp.int32(0), unroll=4)

    def fetch(source, buf, f):
        return pltpu.make_async_copy(source, p_buf.at[buf, f], sems.at[buf, f])

    def fetch_a(e, buf):
        return pltpu.make_async_copy(a_ref.at[e], a_buf.at[buf], sems.at[buf, KC])

    def start(i):
        @pl.when(i < count)
        def _():
            e, buf = picked[i], lax.rem(i, depth)
            fetch_a(e, buf).start()
            fetch(own.at[e], buf, 0).start()
            for f, source in ((1, own), (2, own), (5, left), (6, right)):
                fetch(source.at[near[f - 1, e]], buf, f).start()
            for f, parts in ((4 - odd, first), (3 + odd, second)):
                n = near[f - 1, e]
                for part, at, end in zip(parts, cuts, cuts[1:]):

                    @pl.when((n >= at) & (n < end))
                    def _():
                        fetch(part.at[n - at], buf, f).start()

    for i in range(depth - GROUP):
        start(i)
    acc[...] = jnp.zeros_like(acc)

    def group(g, carry):
        for u in range(GROUP):
            start(g * GROUP + u + depth - GROUP)
        for u in range(GROUP):
            buf = lax.rem(g * GROUP + u, depth)

            @pl.when(g * GROUP + u < count)
            def _():
                fetch_a(0, buf).wait()
                for f in range(KC):
                    fetch(own.at[0], buf, f).wait()

        for u in range(GROUP):
            buf = lax.rem(g * GROUP + u, depth)
            for f in range(KC):
                t_buf[u, :, f * width : (f + 1) * width] = jnp.dot(
                    a_buf[buf, f], p_buf[buf, f], preferred_element_type=jnp.float32
                ).astype(jnp.bfloat16)
        weighted = [
            lax.dot_general(
                p_buf[lax.rem(g * GROUP + u, depth), 0], t_buf[u], (((0,), (0,)), ((), ())),
                preferred_element_type=jnp.float32,
            )
            for u in range(GROUP)
        ]
        for u in range(GROUP):
            i = g * GROUP + u

            @pl.when(i < count)
            def _():
                e = picked[i]
                a = agg[e]
                for f in range(KC):
                    row = a * KC + slot[f, e]
                    acc[row] = acc[row] + weighted[u][:, f * width : (f + 1) * width]

        return carry

    lax.fori_loop(0, (count + GROUP - 1) // GROUP, group, 0)

    def moves(r):
        return [
            pltpu.make_async_copy(halves.at[h, r], out.at[r], out_sems.at[h, r])
            for h, out in ((0, low), (1, high))
        ]

    def store(r, carry):
        for s in range(KC):
            block = acc[r * KC + s].astype(jnp.bfloat16)
            halves[0, r, s] = block[:half]
            halves[1, r, s] = block[half:]
        for move in moves(r):
            move.start()
        return carry

    lax.fori_loop(0, aggs, store, 0)

    def finish(r, carry):
        for move in moves(r):
            move.wait()
        return carry

    lax.fori_loop(0, aggs, finish, 0)


def chunk(distance, aggs, cuts, tables, a_blocks, blocks):
    elems, _, width, _ = a_blocks.shape
    out = jax.ShapeDtypeStruct((aggs, KC, width // 2, width), jnp.bfloat16)
    smem = pl.BlockSpec(memory_space=pltpu.SMEM)
    hbm = pl.BlockSpec(memory_space=pl.ANY)
    depth = 3 * GROUP
    return pl.pallas_call(
        functools.partial(chunk_kernel, distance, cuts),
        out_shape=(out, out),
        in_specs=[smem] * len(tables) + [hbm] * (1 + len(blocks)),
        out_specs=(hbm, hbm),
        scratch_shapes=[
            pltpu.VMEM((aggs * KC, width, width), jnp.float32),
            pltpu.VMEM((depth, KC, width, width), jnp.bfloat16),
            pltpu.VMEM((depth, KC, width, width), jnp.bfloat16),
            pltpu.VMEM((GROUP, width, KC * width), jnp.bfloat16),
            pltpu.VMEM((2, aggs, KC, width // 2, width), jnp.bfloat16),
            pltpu.SMEM((elems + 1,), jnp.int32),
            pltpu.SemaphoreType.DMA((depth, KC + 1)),
            pltpu.SemaphoreType.DMA((2, aggs)),
        ],
        compiler_params=pltpu.CompilerParams(vmem_limit_bytes=VMEM_BYTES),
        cost_estimate=pl.CostEstimate(
            flops=4 * KC * width**3 * 4, bytes_accessed=12 * 1024 * 1024, transcendentals=0
        ),
    )(*tables, a_blocks, *blocks)


def add(*terms):
    return sum(t.astype(jnp.float32) for t in terms).astype(jnp.bfloat16)


def on_device(a_blocks, p_blocks, neighbours, coarse_slot, owner, agg_local):
    elems = p_blocks.shape[0]
    aggs = elems // 4
    count = lax.axis_size("dev")

    order = ring_order(count)
    places = jnp.array([order.index(d) for d in range(count)], jnp.int32)
    tables = (places, owner.T, agg_local, neighbours.T, coarse_slot.T)

    cuts, first, second = halo_dev(p_blocks, count)
    size = lax.axis_size("grp")
    forward = [(i, i + 1) for i in range(size - 1)]
    backward = [(b, a) for a, b in forward]
    left, right = lax.ppermute(p_blocks, "grp", forward), lax.ppermute(p_blocks, "grp", backward)
    blocks = lax.optimization_barrier((p_blocks, *first, *second, left, right))

    chunks = {}

    def part(distance, side):
        distance %= count
        if distance not in chunks:
            chunks[distance] = chunk(distance, aggs, cuts, tables, a_blocks, blocks)
        return chunks[distance][side]

    right = [(order[i], order[(i + 1) % count]) for i in range(count)]
    left = [(b, a) for a, b in right]
    far = count // 2
    got = {}
    for n in range(2 * far - 1):
        distance = far - (n + 1) // 2
        for sign, perm in ((1, right), (-1, left)):
            side = n % 2 if sign > 0 else 1 - n % 2
            terms = [part(sign * distance, side)]
            if n >= 2:
                terms.append(got[sign, n - 2])
            got[sign, n] = lax.ppermute(terms[0] if n < 2 else add(*terms), "dev", perm)
    last = 2 * far - 2
    low = add(part(0, 0), got[1, last], got[-1, last - 1])
    high = add(part(0, 1), got[1, last - 1], got[-1, last])
    return jnp.concatenate([low, high], 2)


def solution(mesh):
    placed = (
        P(("grp", "dev"), None, None, None),
        P(("grp", "dev"), None, None),
        P(("grp", "dev"), None),
        P(("grp", "dev"), None),
        P(("grp", "dev"), None),
        P(("grp", "dev")),
    )
    return jax.shard_map(
        on_device,
        mesh=mesh,
        in_specs=placed,
        out_specs=P(("grp", "dev"), None, None, None),
        check_vma=False,
    )
```

```python
import functools

import jax
import jax.numpy as jnp
from jax import lax
from jax.experimental import pallas as pl
from jax.experimental.pallas import tpu as pltpu
from jax.sharding import PartitionSpec as P

KC = 7
GROUP = 2
VMEM_BYTES = 56 * 1024 * 1024


def columns(count):
    return 1 << ((count.bit_length() - 1) // 2)


def ring_order(count):
    nx = columns(count)
    nz = count // nx
    if nx < 2 or nz < 2 or nz % 2 or nx * nz != count:
        return list(range(count))
    walk = [(z, 0) for z in range(nz)]
    for step, z in enumerate(reversed(range(nz))):
        xs = range(1, nx)
        walk += [(z, x) for x in (xs if step % 2 == 0 else reversed(xs))]
    return [z * nx + x for z, x in walk]


def halo_dev(p_blocks, count):
    if columns(count) != 2:
        forward = [(i, i + 1) for i in range(count - 1)]
        backward = [(b, a) for a, b in forward]
        return (
            (0, p_blocks.shape[0]),
            [lax.ppermute(p_blocks, "dev", backward)],
            [lax.ppermute(p_blocks, "dev", forward)],
        )
    elems = p_blocks.shape[0]
    cuts = (0, 16 * elems // 32, 25 * elems // 32, elems)
    swap = [(i, i ^ 1) for i in range(count)]
    relay = [(i, i + 2) for i in range(0, count - 2, 2)] + [(i, i - 2) for i in range(3, count, 2)]
    straight = [(i, i - 1) for i in range(2, count, 2)] + [(i, i + 1) for i in range(1, count - 1, 2)]
    first, second = [], []
    for low, high in zip(cuts, cuts[1:]):
        piece = p_blocks[low:high]
        if first:
            piece, _ = lax.optimization_barrier((piece, first[-1]))
        first.append(lax.ppermute(piece, "dev", swap))
        if high < elems:
            second.append(lax.ppermute(first[-1], "dev", relay))
        else:
            second.append(lax.ppermute(piece, "dev", straight))
    return cuts, first, second


def chunk_kernel(distance, cuts, places, owner, agg, near, slot, a_ref, own, *refs):
    pieces = len(cuts) - 1
    first, second, (left, right) = refs[:pieces], refs[pieces : 2 * pieces], refs[2 * pieces : 2 * pieces + 2]
    low, high, acc, a_buf, p_buf, t_buf, halves, picked, sems, out_sems = refs[2 * pieces + 2 :]
    elems, count_dev = owner.shape[1], places.shape[0]
    aggs, _, half, width = low.shape
    depth = a_buf.shape[0]
    me = lax.axis_index("dev")
    odd = lax.rem(me, 2) if pieces > 1 else 0
    target = lax.rem(places[me] + distance, count_dev)

    def pick(e, count):
        picked[count] = e
        return count + (places[owner[0, e]] == target).astype(jnp.int32)

    count = lax.fori_loop(0, elems, pick, jnp.int32(0), unroll=4)

    def fetch(source, buf, f):
        return pltpu.make_async_copy(source, p_buf.at[buf, f], sems.at[buf, f])

    def fetch_a(e, buf):
        return pltpu.make_async_copy(a_ref.at[e], a_buf.at[buf], sems.at[buf, KC])

    def start(i):
        @pl.when(i < count)
        def _():
            e, buf = picked[i], lax.rem(i, depth)
            fetch_a(e, buf).start()
            fetch(own.at[e], buf, 0).start()
            for f, source in ((1, own), (2, own), (5, left), (6, right)):
                fetch(source.at[near[f - 1, e]], buf, f).start()
            for f, parts in ((4 - odd, first), (3 + odd, second)):
                n = near[f - 1, e]
                for part, at, end in zip(parts, cuts, cuts[1:]):

                    @pl.when((n >= at) & (n < end))
                    def _():
                        fetch(part.at[n - at], buf, f).start()

    for i in range(depth - GROUP):
        start(i)
    acc[...] = jnp.zeros_like(acc)

    def group(g, carry):
        for u in range(GROUP):
            start(g * GROUP + u + depth - GROUP)
        for u in range(GROUP):
            buf = lax.rem(g * GROUP + u, depth)

            @pl.when(g * GROUP + u < count)
            def _():
                fetch_a(0, buf).wait()
                for f in range(KC):
                    fetch(own.at[0], buf, f).wait()

        for u in range(GROUP):
            buf = lax.rem(g * GROUP + u, depth)
            for f in range(KC):
                t_buf[u, :, f * width : (f + 1) * width] = jnp.dot(
                    a_buf[buf, f], p_buf[buf, f], preferred_element_type=jnp.float32
                ).astype(jnp.bfloat16)
        weighted = [
            lax.dot_general(
                p_buf[lax.rem(g * GROUP + u, depth), 0], t_buf[u], (((0,), (0,)), ((), ())),
                preferred_element_type=jnp.float32,
            )
            for u in range(GROUP)
        ]
        for u in range(GROUP):
            i = g * GROUP + u

            @pl.when(i < count)
            def _():
                e = picked[i]
                a = agg[e]
                for f in range(KC):
                    row = a * KC + slot[f, e]
                    acc[row] = acc[row] + weighted[u][:, f * width : (f + 1) * width]

        return carry

    lax.fori_loop(0, (count + GROUP - 1) // GROUP, group, 0)

    def moves(r):
        return [
            pltpu.make_async_copy(halves.at[h, r], out.at[r], out_sems.at[h, r])
            for h, out in ((0, low), (1, high))
        ]

    def store(r, carry):
        for s in range(KC):
            block = acc[r * KC + s].astype(jnp.bfloat16)
            halves[0, r, s] = block[:half]
            halves[1, r, s] = block[half:]
        for move in moves(r):
            move.start()
        return carry

    lax.fori_loop(0, aggs, store, 0)

    def finish(r, carry):
        for move in moves(r):
            move.wait()
        return carry

    lax.fori_loop(0, aggs, finish, 0)


def chunk(distance, aggs, cuts, tables, a_blocks, blocks):
    elems, _, width, _ = a_blocks.shape
    out = jax.ShapeDtypeStruct((aggs, KC, width // 2, width), jnp.bfloat16)
    smem = pl.BlockSpec(memory_space=pltpu.SMEM)
    hbm = pl.BlockSpec(memory_space=pl.ANY)
    depth = 3 * GROUP
    return pl.pallas_call(
        functools.partial(chunk_kernel, distance, cuts),
        out_shape=(out, out),
        in_specs=[smem] * len(tables) + [hbm] * (1 + len(blocks)),
        out_specs=(hbm, hbm),
        scratch_shapes=[
            pltpu.VMEM((aggs * KC, width, width), jnp.float32),
            pltpu.VMEM((depth, KC, width, width), jnp.bfloat16),
            pltpu.VMEM((depth, KC, width, width), jnp.bfloat16),
            pltpu.VMEM((GROUP, width, KC * width), jnp.bfloat16),
            pltpu.VMEM((2, aggs, KC, width // 2, width), jnp.bfloat16),
            pltpu.SMEM((elems + 1,), jnp.int32),
            pltpu.SemaphoreType.DMA((depth, KC + 1)),
            pltpu.SemaphoreType.DMA((2, aggs)),
        ],
        compiler_params=pltpu.CompilerParams(vmem_limit_bytes=VMEM_BYTES),
        cost_estimate=pl.CostEstimate(
            flops=4 * KC * width**3 * 4, bytes_accessed=12 * 1024 * 1024, transcendentals=0
        ),
    )(*tables, a_blocks, *blocks)


def add(*terms):
    return sum(t.astype(jnp.float32) for t in terms).astype(jnp.bfloat16)


def on_device(a_blocks, p_blocks, neighbours, coarse_slot, owner, agg_local):
    elems = p_blocks.shape[0]
    aggs = elems // 4
    count = lax.axis_size("dev")

    order = ring_order(count)
    places = jnp.array([order.index(d) for d in range(count)], jnp.int32)
    tables = (places, owner.T, agg_local, neighbours.T, coarse_slot.T)

    cuts, first, second = halo_dev(p_blocks, count)
    size = lax.axis_size("grp")
    forward = [(i, i + 1) for i in range(size - 1)]
    backward = [(b, a) for a, b in forward]
    left, right = lax.ppermute(p_blocks, "grp", forward), lax.ppermute(p_blocks, "grp", backward)
    blocks = lax.optimization_barrier((p_blocks, *first, *second, left, right))

    chunks = {}

    def part(distance, side):
        distance %= count
        if distance not in chunks:
            chunks[distance] = chunk(distance, aggs, cuts, tables, a_blocks, blocks)
        return chunks[distance][side]

    right = [(order[i], order[(i + 1) % count]) for i in range(count)]
    left = [(b, a) for a, b in right]
    far = count // 2
    got = {}
    for n in range(2 * far - 1):
        distance = far - (n + 1) // 2
        for sign, perm in ((1, right), (-1, left)):
            side = n % 2 if sign > 0 else 1 - n % 2
            terms = [part(sign * distance, side)]
            if n >= 2:
                terms.append(got[sign, n - 2])
            got[sign, n] = lax.ppermute(terms[0] if n < 2 else add(*terms), "dev", perm)
    last = 2 * far - 2
    low, high = lax.optimization_barrier((add(part(0, 0), got[-1, last - 1]), add(part(0, 1), got[1, last - 1])))
    low, high = add(low, got[1, last]), add(high, got[-1, last])
    return jnp.concatenate([low, high], 2)


def solution(mesh):
    placed = (
        P(("grp", "dev"), None, None, None),
        P(("grp", "dev"), None, None),
        P(("grp", "dev"), None),
        P(("grp", "dev"), None),
        P(("grp", "dev"), None),
        P(("grp", "dev")),
    )
    return jax.shard_map(
        on_device,
        mesh=mesh,
        in_specs=placed,
        out_specs=P(("grp", "dev"), None, None, None),
        check_vma=False,
    )
```
